256 devices in a mesh: branch: 32 (over y, z), tensor: 8 (over x, core).
Axes of the slice: x: 4, y: 4, z: 8, core: 2. Of those that a mesh axis runs over, the one named last changes fastest.
Arguments:
- query: bfloat16 [256, 2, 128, 192], P('branch', None, 'tensor'), may hold values from -52 to 52
- absorb_key: bfloat16 [128, 128, 512], P('tensor'), may hold values from -0.5 to 0.5
- absorb_value: bfloat16 [128, 512, 128], P('tensor'), may hold values from -0.25 to 0.25
- prefix_cache: bfloat16 [2048, 576], replicated, may hold values from -6 to 6
- home_cache: bfloat16 [256, 256, 576], P('branch'), may hold values from -6 to 6
- spill_pool: bfloat16 [1024, 128, 576], P('branch'), may hold values from -6 to 6
- new_latent: bfloat16 [256, 2, 576], P('branch', None, 'tensor'), may hold values from -6 to 6
- lengths: int32 [256], P('branch'), may hold values from 1 to 768, as said below
- spill_table: int32 [256, 4], P('branch'), may hold values from 0 to 1023, as said below
Outputs:
- head_output: bfloat16 [256, 2, 128, 128], P('branch', None, 'tensor')
The draws below stay inside these ranges and needn't reach their ends.
Inputs may be any that keep to these rules, and one draw needn't show every extreme that they name: Every branch has at least one cached suffix token; in every draw some branch has exactly 768. Branch b lies on device d = b // 8 of branch, and its k-th spilled block (for k * 128 < lengths[b] - 256) sits in pool slot h * 32 + d + c of some holder device h and some c < 1; distinct blocks have distinct slots. `spill_table`: entries of blocks beyond a branch's length are valid slot numbers that carry nothing.
All inputs are finite; a program needn't handle non-finite values.
Results may differ from the reference program's by a relative error of at most 0.012.
The reference program's roundings to bfloat16 on the way count: a program that leaves them out, or rounds other values in their place, can miss the bound.
Values may be sent and summed in bfloat16 or wider, within the bound.
A program may use at most 64 MiB of HBM per device.

```python
import jax
import jax.numpy as jnp
from jax import lax

HEADS = 128
NOPE = 128
ROPE = 64
LATENT = 512
VHEAD = 128
BR_DEV = 8
PREFIX = 2048
HOME = 256
BLOCK = 128
CAP = 1
STEPS = 2
BRANCHES = 256
SPB = 4
POOL = 1024


def spill_layout(key):
    dev_count = BRANCHES // BR_DEV
    slot_total = dev_count * CAP
    key_heavy, key_count, key_slots, key_light, key_tail = jax.random.split(key, 5)
    heavy = jax.random.permutation(key_heavy, dev_count) < (dev_count + 1) // 2
    blocks = jax.random.randint(key_count, (dev_count, BR_DEV), (SPB + 1) // 2, SPB + 1)
    blocks = blocks.at[:, 0].set(SPB)
    blocks = jnp.where(heavy[:, None], blocks, 0)
    before = jnp.cumsum(blocks, 1) - blocks
    orders = jax.vmap(lambda sub_key: jax.random.permutation(sub_key, slot_total))(jax.random.split(key_slots, dev_count))
    block_index = jnp.arange(SPB)
    place = jnp.minimum(before[:, :, None] + block_index[None, None, :], slot_total - 1)
    live = block_index[None, None, :] < blocks[:, :, None]
    chosen = orders[jnp.arange(dev_count)[:, None, None], place]
    holder = chosen // CAP
    column = chosen % CAP
    owner = jnp.arange(dev_count)[:, None, None]
    ident = holder * slot_total + owner * CAP + column
    table = jnp.where(live, ident, 0).reshape(BRANCHES, SPB)
    tail = jax.random.randint(key_tail, (dev_count, BR_DEV), 1, BLOCK + 1)
    tail = tail.at[:, 0].set(BLOCK)
    heavy_len = HOME + (blocks - 1) * BLOCK + tail
    light_len = jax.random.randint(key_light, (dev_count, BR_DEV), 1, HOME + 1)
    light_len = light_len.at[:, BR_DEV - 1].set(1)
    length = jnp.where(heavy[:, None], heavy_len, light_len).reshape(BRANCHES)
    return (length.astype(jnp.int32), table.astype(jnp.int32))


def draw_lengths(key, part):
    return spill_layout(key)[0]


def draw_spill_table(key, part):
    return spill_layout(key)[1]


def draw_query(key, part):
    key = jax.random.fold_in(key, 7)
    key_value = jax.random.fold_in(key, 0)
    shape = (BRANCHES, STEPS, HEADS, NOPE + ROPE)
    values = jnp.clip(jax.random.normal(key_value, shape, jnp.float32), -6.0, 6.0)
    return values.astype(jnp.bfloat16)


def steps_of(stream_key, shape, shards, least, top_value):
    level, own = 1.0, jax.random.fold_in(stream_key, 6)
    for position, blocks in shards:
        draws = jnp.exp(jax.random.uniform(jax.random.fold_in(own, position), (blocks,), jnp.float32, least / len(shards), top_value / len(shards)))
        level = level * jnp.repeat(draws, shape[position] // blocks).reshape([-1 if axis == position else 1 for axis in range(len(shape))])
    return level


def scatter_about(own_key, dims, width, limit, pieces=(), dtype=jnp.bfloat16):
    loudness = steps_of(own_key, dims, pieces, -0.22, 0.18) if pieces else 1.0
    entries = jax.random.normal(own_key, dims, jnp.float32) * width * loudness
    return jnp.minimum(jnp.maximum(entries, -limit), limit).astype(dtype)


def setup_inputs(seed: int = 0) -> dict:
    streams_of = jax.random.split(jax.random.key(seed), 10)
    return {
        "query": draw_query(jax.random.fold_in(streams_of[9], 71), 0),
        "absorb_key": scatter_about(streams_of[1], (HEADS, NOPE, LATENT), NOPE ** -0.5, 0.5, ((0, 8),)),
        "absorb_value": scatter_about(streams_of[2], (HEADS, LATENT, VHEAD), LATENT ** -0.5, 0.25, ((0, 8),)),
        "prefix_cache": scatter_about(streams_of[3], (PREFIX, LATENT + ROPE), 1.0, 6.0),
        "home_cache": scatter_about(streams_of[4], (BRANCHES, HOME, LATENT + ROPE), 1.0, 6.0, ((0, 32),)),
        "spill_pool": scatter_about(streams_of[5], (POOL, BLOCK, LATENT + ROPE), 1.0, 6.0, ((0, 32),)),
        "new_latent": scatter_about(streams_of[6], (BRANCHES, STEPS, LATENT + ROPE), 1.0, 6.0, ((0, 32), (2, 8))),
        "lengths": draw_lengths(jax.random.fold_in(streams_of[9], 71), 0),
        "spill_table": draw_spill_table(jax.random.fold_in(streams_of[9], 71), 0),
    }


def reference(query, absorb_key, absorb_value, prefix_cache, home_cache, spill_pool, new_latent, lengths, spill_table):
    score_scale = (NOPE + ROPE) ** -0.5
    latent_query = jnp.einsum('bshn,hnl->bshl', query[..., :NOPE].astype(jnp.float32), absorb_key.astype(jnp.float32)).astype(jnp.bfloat16)
    full_query = jnp.concatenate([latent_query, query[..., NOPE:]], -1)

    def one_branch(packed):
        branch_query, home_rows, table_row, length, fresh = packed
        spilled = spill_pool[table_row].reshape(SPB * BLOCK, LATENT + ROPE)
        keys_all = jnp.concatenate([prefix_cache, home_rows, spilled, fresh], 0).astype(jnp.float32)
        base_mask = jnp.concatenate([
            jnp.ones((PREFIX,), bool),
            jnp.arange(HOME) < length,
            jnp.arange(SPB * BLOCK) < length - HOME])
        fresh_mask = jnp.arange(STEPS)[None, :] <= jnp.arange(STEPS)[:, None]
        full_mask = jnp.concatenate([jnp.broadcast_to(base_mask[None, :], (STEPS, base_mask.shape[0])), fresh_mask], 1)
        scores = jnp.einsum('shk,tk->sht', branch_query.astype(jnp.float32), keys_all) * score_scale
        scores = jnp.where(full_mask[:, None, :], scores, -jnp.inf)
        weights = jax.nn.softmax(scores, -1)
        latent_out = jnp.einsum('sht,tl->shl', weights, keys_all[:, :LATENT])
        return latent_out.astype(jnp.bfloat16)

    latent_all = lax.map(one_branch, (full_query, home_cache, spill_table, lengths, new_latent))
    head_output = jnp.einsum('bshl,hlv->bshv', latent_all.astype(jnp.float32), absorb_value.astype(jnp.float32))
    return head_output.astype(jnp.bfloat16)
```

```python
import functools
import math

import jax
import jax.numpy as jnp
from jax import lax
from jax.experimental import pallas as pl
from jax.experimental.pallas import tpu as pltpu
from jax.sharding import PartitionSpec as P

MESH = pl.DeviceIdType.MESH
FLOOR = -1e30
KEY_TILE = 512


def nt_dot(a, b):
    return lax.dot_general(a, b, (((1,), (1,)), ((), ())), preferred_element_type=jnp.float32)


def attention_kernel(
    dims,
    query_ref,
    wk_ref,
    wv_ref,
    prefix_ref,
    home_ref,
    pool_ref,
    fresh_ref,
    len_ref,
    table_ref,
    out_ref,
    q_buf,
    wk_buf,
    wv_buf,
    prefix_buf,
    home_buf,
    new_buf,
    spill,
    flat_buf,
    lat_buf,
    full_send,
    full_recv,
    fresh_send,
    fresh_recv,
    peak_buf,
    mass_buf,
    acc_buf,
    lo_send,
    lo_recv,
    out_buf,
    local_sem,
    q_send_sem,
    q_recv_sem,
    f_send_sem,
    f_recv_sem,
    s_send_sem,
    s_recv_sem,
    x_send_sem,
    x_recv_sem,
    o_send_sem,
    o_recv_sem,
    *chunk_bufs,
):
    n_dev, n_ten, branches, steps, heads, nope, rope, latent, home, block, per_branch, chunks = dims
    width = latent + rope
    rows = steps * heads
    bs = branches * steps
    all_rows = n_ten * rows
    n_chunk = len(chunks)
    pair_rows = 2 * width // n_ten
    even_rows = sum(wide[0] for wide in chunks)
    pool_recv = chunk_bufs[:n_chunk]
    stage = chunk_bufs[n_chunk:]
    me = lax.axis_index("branch")
    mine = lax.axis_index("tensor")
    scale = (nope + rope) ** -0.5 / math.log(2.0)

    def dev(i):
        return lax.rem(me + i, n_dev)

    def ten(i):
        return lax.rem(mine + i, n_ten)

    barrier = pltpu.get_barrier_semaphore()

    def greet_dev(i, carry):
        pl.semaphore_signal(barrier, inc=1, device_id={"branch": dev(i)}, device_id_type=MESH)
        return carry

    def greet_ten(i, carry):
        pl.semaphore_signal(barrier, inc=1, device_id={"tensor": ten(i)}, device_id_type=MESH)
        return carry

    lax.fori_loop(1, n_dev, greet_dev, 0)
    lax.fori_loop(1, n_ten, greet_ten, 0)

    def rows_of(t, odd, c):
        first = sum(wide[odd] for wide in chunks[:c]) + odd * even_rows
        return pl.ds(pl.multiple_of(t // 2 * pair_rows + first, 16), chunks[c][odd])

    def by_parity(body):
        for odd in range(2):
            pl.when(lax.rem(mine, 2) == odd)(functools.partial(body, odd))

    locals_ = [
        pltpu.make_async_copy(query_ref, q_buf, local_sem.at[0]),
        pltpu.make_async_copy(wk_ref, wk_buf, local_sem.at[1]),
        pltpu.make_async_copy(prefix_ref, prefix_buf, local_sem.at[2]),
        pltpu.make_async_copy(home_ref.at[mine], home_buf, local_sem.at[3]),
        pltpu.make_async_copy(wv_ref, wv_buf, local_sem.at[4]),
    ]
    for copy in locals_:
        copy.start()

    def own_copy(odd, c):
        return pltpu.make_async_copy(
            pool_ref.at[me, rows_of(mine, odd, c)],
            pool_recv[c].at[me, pl.ds(0, chunks[c][odd])],
            local_sem.at[5 + c],
        )

    def block_copy(i, odd, c, source, target):
        return pltpu.make_async_remote_copy(
            src_ref=pool_ref.at[target, rows_of(mine, odd, c)],
            dst_ref=pool_recv[c].at[source, pl.ds(0, chunks[c][odd])],
            send_sem=s_send_sem.at[c, i],
            recv_sem=s_recv_sem.at[c, i],
            device_id={"branch": target},
            device_id_type=MESH,
        )

    pl.semaphore_wait(barrier, n_dev - 1 + n_ten - 1)

    @by_parity
    def _(odd):
        for c in range(n_chunk):

            def send_block(i, carry, c=c):
                block_copy(i, odd, c, me, dev(i)).start()
                return carry

            lax.fori_loop(1, n_dev, send_block, 0)
            own_copy(odd, c).start()

    locals_[0].wait()
    q_flat = q_buf[...].reshape(bs * heads, nope + rope).astype(jnp.float32)
    flat_buf[0, :, pl.ds(0, nope)] = q_flat[:, :nope]
    flat_buf[1, :, pl.ds(0, rope)] = q_flat[:, nope:]
    locals_[1].wait()
    tiles = latent // 128
    for h in range(heads):
        q_head = flat_buf[0, pl.ds(h, bs, stride=heads), :][:, :nope]
        lat_head = jnp.dot(
            q_head.astype(jnp.bfloat16), wk_buf[h], preferred_element_type=jnp.float32
        )
        for j in range(tiles):
            lat_buf[j, pl.ds(h * bs, bs), :] = lat_head[:, j * 128 : (j + 1) * 128]
        lat_buf[tiles, pl.ds(h * bs, bs), :] = flat_buf[1, pl.ds(h, bs, stride=heads), :]
    for b in range(branches):
        for s in range(steps):
            for j in range(tiles + 1):
                wide = 128 if j < tiles else rope
                full_send[b, pl.ds(s * heads, heads), pl.ds(j * 128, wide)] = lat_buf[
                    j, pl.ds(b * steps + s, heads, stride=bs), :
                ][:, :wide].astype(jnp.bfloat16)
    part = width // n_ten
    fresh_send[...] = jnp.zeros_like(fresh_send)
    for b in range(branches):
        fresh_send[b, pl.ds(0, steps), pl.ds(0, part)] = fresh_ref[b]

    def full_copy(i, source, target):
        return pltpu.make_async_remote_copy(
            src_ref=full_send.at[target],
            dst_ref=full_recv.at[source],
            send_sem=q_send_sem.at[i],
            recv_sem=q_recv_sem.at[i],
            device_id={"tensor": target},
            device_id_type=MESH,
        )

    def fresh_copy(i, source, target):
        return pltpu.make_async_remote_copy(
            src_ref=fresh_send.at[target],
            dst_ref=fresh_recv.at[source],
            send_sem=f_send_sem.at[i],
            recv_sem=f_recv_sem.at[i],
            device_id={"tensor": target},
            device_id_type=MESH,
        )

    for i in range(1, n_ten):
        full_copy(i, mine, ten(i)).start()
        fresh_copy(i, mine, ten(i)).start()
    full_recv[mine] = full_send[mine]
    fresh_recv[mine] = fresh_send[mine]
    for i in range(1, n_ten):
        full_copy(i, ten(n_ten - i), mine).wait_recv()
        fresh_copy(i, ten(n_ten - i), mine).wait_recv()

    fresh_all = jnp.zeros((fresh_recv.shape[1], width + fresh_recv.shape[2]), jnp.float32)
    for t in range(n_ten):
        piece = fresh_recv[t].astype(jnp.float32)
        piece = jnp.concatenate([piece, jnp.zeros((piece.shape[0], width), jnp.float32)], 1)
        fresh_all = fresh_all + (pltpu.roll(piece, t * part, 1) if t else piece)
    new_buf[...] = jnp.zeros_like(new_buf)
    new_buf[pl.ds(0, fresh_recv.shape[1]), :] = fresh_all[:, :width].astype(jnp.bfloat16)

    queries = full_recv[...].reshape(all_rows, width)
    length = len_ref[mine]

    def attend(scores, combine):
        peak_old = peak_buf[...]
        peak = jnp.maximum(peak_old, jnp.max(scores, 1, keepdims=True))
        weights = jnp.exp2(scores - peak)
        factor = jnp.exp2(peak_old - peak)
        mass_buf[...] = mass_buf[...] * factor + jnp.sum(weights, 1, keepdims=True)
        peak_buf[...] = peak
        acc_buf[...] = acc_buf[...] * factor + combine(weights.astype(jnp.bfloat16))

    def attend_columns(keys, bound):
        scores = jnp.dot(queries, keys, preferred_element_type=jnp.float32) * scale
        if bound is not None:
            column = lax.broadcasted_iota(jnp.int32, scores.shape, 1)
            scores = jnp.where(column < bound, scores, FLOOR)
        attend(scores, lambda weights: nt_dot(weights, keys[:latent]))

    peak_buf[...] = jnp.full_like(peak_buf, FLOOR)
    mass_buf[...] = jnp.zeros_like(mass_buf)
    acc_buf[...] = jnp.zeros_like(acc_buf)
    locals_[2].wait()

    def prefix_tile(j, carry):
        attend_columns(prefix_buf[:, pl.ds(pl.multiple_of(j * KEY_TILE, KEY_TILE), KEY_TILE)], None)
        return carry

    lax.fori_loop(0, prefix_buf.shape[1] // KEY_TILE, prefix_tile, 0)

    locals_[3].wait()
    attend_columns(home_buf[...], length)
    keys = new_buf[...]
    scores = nt_dot(queries, keys) * scale
    column = lax.broadcasted_iota(jnp.int32, scores.shape, 1)
    row_step = lax.broadcasted_iota(jnp.int32, scores.shape, 0) // heads % steps
    attend(
        jnp.where(column <= row_step, scores, FLOOR),
        lambda weights: jnp.dot(weights, keys[:, :latent], preferred_element_type=jnp.float32),
    )

    def regroup_copy(i, odd, c, source, target):
        return pltpu.make_async_remote_copy(
            src_ref=stage[c].at[target, pl.ds(0, chunks[c][odd])],
            dst_ref=spill.at[rows_of(source, odd, c)],
            send_sem=x_send_sem.at[c, i],
            recv_sem=x_recv_sem.at[c, i],
            device_id={"tensor": target},
            device_id_type=MESH,
        )

    @by_parity
    def _(odd):
        for c in range(n_chunk):

            def wait_block(i, carry, c=c):
                block_copy(i, odd, c, dev(n_dev - i), me).wait_recv()
                return carry

            lax.fori_loop(1, n_dev, wait_block, 0)
            own_copy(odd, c).wait()
            some = pl.ds(0, chunks[c][odd])
            for i in range(1, n_ten):
                target = ten(i)
                for k in range(per_branch):
                    holder = table_ref[k, target] // n_dev
                    stage[c][target, some, pl.ds(k * block, block)] = pool_recv[c][holder, some, :]
                regroup_copy(i, odd, c, mine, target).start()
            for k in range(per_branch):
                holder = table_ref[k, mine] // n_dev
                spill[rows_of(mine, odd, c), pl.ds(k * block, block)] = pool_recv[c][
                    holder, some, :
                ]
        for c in range(n_chunk):
            for i in range(1, n_ten):
                regroup_copy(i, (odd + i) % 2, c, ten(n_ten - i), mine).wait_recv()

    attend_columns(spill[...], length - home)

    lo_send[...] = (acc_buf[...] / mass_buf[...]).astype(jnp.bfloat16).reshape(lo_send.shape)

    def back_copy(i, source, target):
        return pltpu.make_async_remote_copy(
            src_ref=lo_send.at[target],
            dst_ref=lo_recv.at[source],
            send_sem=o_send_sem.at[i],
            recv_sem=o_recv_sem.at[i],
            device_id={"tensor": target},
            device_id_type=MESH,
        )

    for i in range(1, n_ten):
        back_copy(i, mine, ten(i)).start()
    lo_recv[mine] = lo_send[mine]
    locals_[4].wait()
    for i in range(1, n_ten):
        back_copy(i, ten(n_ten - i), mine).wait_recv()
    for j in range(tiles):
        lat_buf[j] = (
            lo_recv[:, :, pl.ds(j * 128, 128)].reshape(branches * rows, 128).astype(jnp.float32)
        )
    for h in range(heads):
        head_rows = jnp.concatenate(
            [lat_buf[j, pl.ds(h, bs, stride=heads), :] for j in range(tiles)], 1
        ).astype(jnp.bfloat16)
        out_buf[pl.ds(h, bs, stride=heads), :] = jnp.dot(
            head_rows, wv_buf[h], preferred_element_type=jnp.float32
        )
    out_ref[...] = out_buf[...].reshape(out_ref.shape).astype(jnp.bfloat16)

    @by_parity
    def _(odd):
        for c in range(n_chunk):

            def sent_block(i, carry, c=c):
                block_copy(i, odd, c, me, dev(i)).wait_send()
                return carry

            lax.fori_loop(1, n_dev, sent_block, 0)
            for i in range(1, n_ten):
                regroup_copy(i, odd, c, mine, ten(i)).wait_send()

    for i in range(1, n_ten):
        full_copy(i, mine, ten(i)).wait_send()
        fresh_copy(i, mine, ten(i)).wait_send()
        back_copy(i, mine, ten(i)).wait_send()


def per_device(
    query,
    absorb_key,
    absorb_value,
    prefix_cache,
    home_cache,
    spill_pool,
    new_latent,
    lengths,
    spill_table,
):
    branches, steps, heads, q_width = query.shape
    nope, latent = absorb_key.shape[1:]
    v_width = absorb_value.shape[2]
    rope = q_width - nope
    width = latent + rope
    home = home_cache.shape[1]
    block = spill_pool.shape[1]
    n_dev = lax.axis_size("branch")
    n_ten = lax.axis_size("tensor")
    per_branch = spill_table.shape[1]
    units = 2 * width // n_ten // 16
    chunks = (((units + 1) // 2 * 16, units // 2 * 16),)
    dims = (
        n_dev, n_ten, branches, steps, heads, nope, rope, latent, home, block, per_branch, chunks
    )
    rows = steps * heads
    bs = branches * steps
    bf16, f32 = jnp.bfloat16, jnp.float32
    hbm = pl.BlockSpec(memory_space=pltpu.HBM)
    smem = pl.BlockSpec(memory_space=pltpu.SMEM)
    vmem = pl.BlockSpec(memory_space=pltpu.VMEM)
    dma = pltpu.SemaphoreType.DMA
    n_chunk = len(chunks)
    out = pl.pallas_call(
        functools.partial(attention_kernel, dims),
        out_shape=jax.ShapeDtypeStruct((bs, heads, v_width), bf16),
        in_specs=[hbm, hbm, hbm, hbm, hbm, hbm, vmem, smem, smem],
        out_specs=vmem,
        scratch_shapes=[
            pltpu.VMEM((bs, heads, q_width), bf16),
            pltpu.VMEM(absorb_key.shape, bf16),
            pltpu.VMEM(absorb_value.shape, bf16),
            pltpu.VMEM(prefix_cache.shape[::-1], bf16),
            pltpu.VMEM((width, home), bf16),
            pltpu.VMEM((128, width), bf16),
            pltpu.VMEM((width, per_branch * block), bf16),
            pltpu.VMEM((2, bs * heads, 128), f32),
            pltpu.VMEM((latent // 128 + 1, bs * heads, 128), f32),
            pltpu.VMEM((branches, rows, width), bf16),
            pltpu.VMEM((n_ten, rows, width), bf16),
            pltpu.VMEM((branches, 16, 128), bf16),
            pltpu.VMEM((n_ten, 16, 128), bf16),
            pltpu.VMEM((n_ten * rows, 1), f32),
            pltpu.VMEM((n_ten * rows, 1), f32),
            pltpu.VMEM((n_ten * rows, latent), f32),
            pltpu.VMEM((n_ten, rows, latent), bf16),
            pltpu.VMEM((branches, rows, latent), bf16),
            pltpu.VMEM((bs * heads, v_width), f32),
            dma((5 + n_chunk,)),
            dma((n_ten,)),
            dma((n_ten,)),
            dma((n_ten,)),
            dma((n_ten,)),
            dma((n_chunk, n_dev)),
            dma((n_chunk, n_dev)),
            dma((n_chunk, n_ten)),
            dma((n_chunk, n_ten)),
            dma((n_ten,)),
            dma((n_ten,)),
        ]
        + [pltpu.VMEM((n_dev, wide[0], block), bf16) for wide in chunks]
        + [pltpu.VMEM((branches, wide[0], per_branch * block), bf16) for wide in chunks],
        compiler_params=pltpu.CompilerParams(
            collective_id=0, has_side_effects=True, vmem_limit_bytes=60 * 1024 * 1024
        ),
    )(
        query.reshape(bs, heads, q_width),
        absorb_key,
        absorb_value,
        prefix_cache.T,
        home_cache.swapaxes(1, 2),
        spill_pool.swapaxes(1, 2),
        new_latent,
        lengths,
        spill_table.T,
    )
    return out.reshape(branches, steps, heads, v_width)


def solution(mesh):
    in_specs = (
        P("branch", None, "tensor", None),
        P("tensor", None, None),
        P("tensor", None, None),
        P(),
        P("branch", None, None),
        P("branch", None, None),
        P("branch", None, "tensor"),
        P("branch"),
        P("branch", None),
    )
    out_specs = P("branch", None, "tensor", None)
    return jax.shard_map(
        per_device, mesh=mesh, in_specs=in_specs, out_specs=out_specs, check_vma=False
    )
```

```python
import functools
import math

import jax
import jax.numpy as jnp
from jax import lax
from jax.experimental import pallas as pl
from jax.experimental.pallas import tpu as pltpu
from jax.sharding import PartitionSpec as P

MESH = pl.DeviceIdType.MESH
FLOOR = -1e30
KEY_TILE = 512


def nt_dot(a, b):
    return lax.dot_general(a, b, (((1,), (1,)), ((), ())), preferred_element_type=jnp.float32)


def attention_kernel(
    dims,
    query_ref,
    wk_ref,
    wv_ref,
    prefix_ref,
    home_ref,
    pool_ref,
    fresh_hbm,
    len_hbm,
    table_hbm,
    out_ref,
    fresh_ref,
    len_ref,
    table_ref,
    q_buf,
    wk_buf,
    wv_buf,
    prefix_buf,
    home_buf,
    new_buf,
    spill,
    flat_buf,
    lat_buf,
    full_send,
    full_recv,
    fresh_send,
    fresh_recv,
    peak_buf,
    mass_buf,
    acc_buf,
    lo_send,
    lo_recv,
    out_buf,
    local_sem,
    q_send_sem,
    q_recv_sem,
    f_send_sem,
    f_recv_sem,
    s_send_sem,
    s_recv_sem,
    x_send_sem,
    x_recv_sem,
    o_send_sem,
    o_recv_sem,
    *chunk_bufs,
):
    n_dev, n_ten, branches, steps, heads, nope, rope, latent, home, block, per_branch, chunks = dims
    width = latent + rope
    rows = steps * heads
    bs = branches * steps
    all_rows = n_ten * rows
    n_chunk = len(chunks)
    pair_rows = 2 * width // n_ten
    even_rows = sum(wide[0] for wide in chunks)
    pool_recv = chunk_bufs[:n_chunk]
    stage = chunk_bufs[n_chunk:]
    me = lax.axis_index("branch")
    mine = lax.axis_index("tensor")
    scale = (nope + rope) ** -0.5 / math.log(2.0)

    def dev(i):
        return lax.rem(me + i, n_dev)

    def ten(i):
        return lax.rem(mine + i, n_ten)

    barrier = pltpu.get_barrier_semaphore()

    def greet_dev(i, carry):
        pl.semaphore_signal(barrier, inc=1, device_id={"branch": dev(i)}, device_id_type=MESH)
        return carry

    def greet_ten(i, carry):
        pl.semaphore_signal(barrier, inc=1, device_id={"tensor": ten(i)}, device_id_type=MESH)
        return carry

    lax.fori_loop(1, n_dev, greet_dev, 0)
    lax.fori_loop(1, n_ten, greet_ten, 0)

    def rows_of(t, odd, c):
        first = sum(wide[odd] for wide in chunks[:c]) + odd * even_rows
        return pl.ds(pl.multiple_of(t // 2 * pair_rows + first, 16), chunks[c][odd])

    def by_parity(body):
        for odd in range(2):
            pl.when(lax.rem(mine, 2) == odd)(functools.partial(body, odd))

    locals_ = [
        pltpu.make_async_copy(query_ref, q_buf, local_sem.at[0]),
        pltpu.make_async_copy(wk_ref, wk_buf, local_sem.at[1]),
        pltpu.make_async_copy(prefix_ref, prefix_buf, local_sem.at[2]),
        pltpu.make_async_copy(home_ref.at[mine], home_buf, local_sem.at[3]),
        pltpu.make_async_copy(wv_ref, wv_buf, local_sem.at[4]),
        pltpu.make_async_copy(fresh_hbm, fresh_ref, local_sem.at[5]),
        pltpu.make_async_copy(len_hbm, len_ref, local_sem.at[6]),
        pltpu.make_async_copy(table_hbm, table_ref, local_sem.at[7]),
    ]
    for copy in locals_:
        copy.start()

    def own_copy(odd, c):
        return pltpu.make_async_copy(
            pool_ref.at[me, rows_of(mine, odd, c)],
            pool_recv[c].at[me, pl.ds(0, chunks[c][odd])],
            local_sem.at[8 + c],
        )

    def all_blocks(odd, c, sem):
        landed = pool_recv[c].at[pl.ds(0, n_dev - 1), pl.ds(0, chunks[c][odd])]
        return pltpu.make_async_copy(landed, landed, sem.at[c])

    def block_copy(odd, c, source, target):
        return pltpu.make_async_remote_copy(
            src_ref=pool_ref.at[target, rows_of(mine, odd, c)],
            dst_ref=pool_recv[c].at[source, pl.ds(0, chunks[c][odd])],
            send_sem=s_send_sem.at[c],
            recv_sem=s_recv_sem.at[c],
            device_id={"branch": target},
            device_id_type=MESH,
        )

    locals_[0].wait()
    q_flat = q_buf[...].reshape(bs * heads, nope + rope).astype(jnp.float32)
    flat_buf[0, :, pl.ds(0, nope)] = q_flat[:, :nope]
    flat_buf[1, :, pl.ds(0, rope)] = q_flat[:, nope:]
    locals_[1].wait()
    tiles = latent // 128
    for h in range(heads):
        q_head = flat_buf[0, pl.ds(h, bs, stride=heads), :][:, :nope]
        lat_head = jnp.dot(
            q_head.astype(jnp.bfloat16), wk_buf[h], preferred_element_type=jnp.float32
        )
        for j in range(tiles):
            lat_buf[j, pl.ds(h * bs, bs), :] = lat_head[:, j * 128 : (j + 1) * 128]
        lat_buf[tiles, pl.ds(h * bs, bs), :] = flat_buf[1, pl.ds(h, bs, stride=heads), :]
    for b in range(branches):
        for s in range(steps):
            for j in range(tiles + 1):
                wide = 128 if j < tiles else rope
                full_send[b, pl.ds(s * heads, heads), pl.ds(j * 128, wide)] = lat_buf[
                    j, pl.ds(b * steps + s, heads, stride=bs), :
                ][:, :wide].astype(jnp.bfloat16)
    part = width // n_ten
    fresh_send[...] = jnp.zeros_like(fresh_send)
    locals_[5].wait()
    for b in range(branches):
        fresh_send[b, pl.ds(0, steps), pl.ds(0, part)] = fresh_ref[b]

    pl.semaphore_wait(barrier, n_dev - 1 + n_ten - 1)

    def full_copy(i, source, target):
        return pltpu.make_async_remote_copy(
            src_ref=full_send.at[target],
            dst_ref=full_recv.at[source],
            send_sem=q_send_sem.at[i],
            recv_sem=q_recv_sem.at[i],
            device_id={"tensor": target},
            device_id_type=MESH,
        )

    def fresh_copy(i, source, target):
        return pltpu.make_async_remote_copy(
            src_ref=fresh_send.at[target],
            dst_ref=fresh_recv.at[source],
            send_sem=f_send_sem.at[i],
            recv_sem=f_recv_sem.at[i],
            device_id={"tensor": target},
            device_id_type=MESH,
        )

    def send_blocks(chosen):
        @by_parity
        def _(odd):
            for c in chosen:

                def send_block(i, carry, c=c):
                    block_copy(odd, c, me, dev(i)).start()
                    return carry

                lax.fori_loop(1, n_dev, send_block, 0)
                own_copy(odd, c).start()

    send_blocks(range(1))
    for i in range(1, n_ten):
        full_copy(i, mine, ten(i)).start()
        fresh_copy(i, mine, ten(i)).start()
    full_recv[mine] = full_send[mine]
    fresh_recv[mine] = fresh_send[mine]
    send_blocks(range(1, n_chunk))

    for i in range(1, n_ten):
        full_copy(i, ten(n_ten - i), mine).wait_recv()
        fresh_copy(i, ten(n_ten - i), mine).wait_recv()

    fresh_all = jnp.zeros((fresh_recv.shape[1], width + fresh_recv.shape[2]), jnp.float32)
    for t in range(n_ten):
        piece = fresh_recv[t].astype(jnp.float32)
        piece = jnp.concatenate([piece, jnp.zeros((piece.shape[0], width), jnp.float32)], 1)
        fresh_all = fresh_all + (pltpu.roll(piece, t * part, 1) if t else piece)
    new_buf[...] = jnp.zeros_like(new_buf)
    new_buf[pl.ds(0, fresh_recv.shape[1]), :] = fresh_all[:, :width].astype(jnp.bfloat16)

    queries = full_recv[...].reshape(all_rows, width)
    locals_[6].wait()
    locals_[7].wait()
    length = len_ref[mine]

    def attend(scores, combine):
        peak_old = peak_buf[...]
        peak = jnp.maximum(peak_old, jnp.max(scores, 1, keepdims=True))
        weights = jnp.exp2(scores - peak)
        factor = jnp.exp2(peak_old - peak)
        mass_buf[...] = mass_buf[...] * factor + jnp.sum(weights, 1, keepdims=True)
        peak_buf[...] = peak
        acc_buf[...] = acc_buf[...] * factor + combine(weights.astype(jnp.bfloat16))

    def attend_columns(keys, bound):
        scores = jnp.dot(queries, keys, preferred_element_type=jnp.float32) * scale
        if bound is not None:
            column = lax.broadcasted_iota(jnp.int32, scores.shape, 1)
            scores = jnp.where(column < bound, scores, FLOOR)
        attend(scores, lambda weights: nt_dot(weights, keys[:latent]))

    peak_buf[...] = jnp.full_like(peak_buf, FLOOR)
    mass_buf[...] = jnp.zeros_like(mass_buf)
    acc_buf[...] = jnp.zeros_like(acc_buf)
    locals_[2].wait()

    def prefix_tile(j, carry):
        attend_columns(prefix_buf[:, pl.ds(pl.multiple_of(j * KEY_TILE, KEY_TILE), KEY_TILE)], None)
        return carry

    lax.fori_loop(0, prefix_buf.shape[1] // KEY_TILE, prefix_tile, 0)

    def regroup_copy(i, odd, c, source, target):
        return pltpu.make_async_remote_copy(
            src_ref=stage[c].at[target, pl.ds(0, chunks[c][odd])],
            dst_ref=spill.at[rows_of(source, odd, c)],
            send_sem=x_send_sem.at[c, i],
            recv_sem=x_recv_sem.at[c, i],
            device_id={"tensor": target},
            device_id_type=MESH,
        )

    def regroup(chosen):
        @by_parity
        def _(odd):
            for c in chosen:

                all_blocks(odd, c, s_recv_sem).wait()
                own_copy(odd, c).wait()
                some = pl.ds(0, chunks[c][odd])
                for i in range(1, n_ten):
                    target = ten(i)
                    for k in range(per_branch):
                        holder = table_ref[k, target] // n_dev
                        stage[c][target, some, pl.ds(k * block, block)] = pool_recv[c][holder, some, :]
                    regroup_copy(i, odd, c, mine, target).start()
                for k in range(per_branch):
                    holder = table_ref[k, mine] // n_dev
                    spill[rows_of(mine, odd, c), pl.ds(k * block, block)] = pool_recv[c][
                        holder, some, :
                    ]

    regroup(range(n_chunk - 1))

    locals_[3].wait()
    attend_columns(home_buf[...], length)
    keys = new_buf[...]
    scores = nt_dot(queries, keys) * scale
    column = lax.broadcasted_iota(jnp.int32, scores.shape, 1)
    row_step = lax.broadcasted_iota(jnp.int32, scores.shape, 0) // heads % steps
    attend(
        jnp.where(column <= row_step, scores, FLOOR),
        lambda weights: jnp.dot(weights, keys[:, :latent], preferred_element_type=jnp.float32),
    )

    regroup(range(n_chunk - 1, n_chunk))

    @by_parity
    def _(odd):
        for c in range(n_chunk):
            for i in range(1, n_ten):
                regroup_copy(i, (odd + i) % 2, c, ten(n_ten - i), mine).wait_recv()

    attend_columns(spill[...], length - home)

    lo_send[...] = (acc_buf[...] * (1.0 / mass_buf[...])).astype(jnp.bfloat16).reshape(lo_send.shape)

    def all_back(sem):
        landed = lo_recv.at[pl.ds(0, n_ten - 1)]
        return pltpu.make_async_copy(landed, landed, sem)

    def back_copy(source, target):
        return pltpu.make_async_remote_copy(
            src_ref=lo_send.at[target],
            dst_ref=lo_recv.at[source],
            send_sem=o_send_sem,
            recv_sem=o_recv_sem,
            device_id={"tensor": target},
            device_id_type=MESH,
        )

    for i in range(1, n_ten):
        back_copy(mine, ten(i)).start()
    lo_recv[mine] = lo_send[mine]
    @by_parity
    def _(odd):
        for c in range(n_chunk):

            all_blocks(odd, c, s_send_sem).wait()
            for i in range(1, n_ten):
                regroup_copy(i, odd, c, mine, ten(i)).wait_send()

    for i in range(1, n_ten):
        full_copy(i, mine, ten(i)).wait_send()
        fresh_copy(i, mine, ten(i)).wait_send()

    locals_[4].wait()
    all_back(o_recv_sem).wait()
    for j in range(tiles):
        lat_buf[j] = (
            lo_recv[:, :, pl.ds(j * 128, 128)].reshape(branches * rows, 128).astype(jnp.float32)
        )
    for h in range(heads):
        head_rows = jnp.concatenate(
            [lat_buf[j, pl.ds(h, bs, stride=heads), :] for j in range(tiles)], 1
        ).astype(jnp.bfloat16)
        out_buf[pl.ds(h, bs, stride=heads), :] = jnp.dot(
            head_rows, wv_buf[h], preferred_element_type=jnp.float32
        )
    out_ref[...] = out_buf[...].reshape(out_ref.shape).astype(jnp.bfloat16)

    all_back(o_send_sem).wait()


def per_device(
    query,
    absorb_key,
    absorb_value,
    prefix_cache,
    home_cache,
    spill_pool,
    new_latent,
    lengths,
    spill_table,
):
    branches, steps, heads, q_width = query.shape
    nope, latent = absorb_key.shape[1:]
    v_width = absorb_value.shape[2]
    rope = q_width - nope
    width = latent + rope
    home = home_cache.shape[1]
    block = spill_pool.shape[1]
    n_dev = lax.axis_size("branch")
    n_ten = lax.axis_size("tensor")
    per_branch = spill_table.shape[1]
    chunks = ((48, 48), (32, 16))
    dims = (
        n_dev, n_ten, branches, steps, heads, nope, rope, latent, home, block, per_branch, chunks
    )
    rows = steps * heads
    bs = branches * steps
    bf16, f32 = jnp.bfloat16, jnp.float32
    hbm = pl.BlockSpec(memory_space=pltpu.HBM)
    vmem = pl.BlockSpec(memory_space=pltpu.VMEM)
    dma = pltpu.SemaphoreType.DMA
    n_chunk = len(chunks)
    out = pl.pallas_call(
        functools.partial(attention_kernel, dims),
        out_shape=pltpu.VMEM((bs, heads, v_width), bf16),
        in_specs=[hbm] * 9,
        out_specs=vmem,
        scratch_shapes=[
            pltpu.VMEM(new_latent.shape, bf16),
            pltpu.SMEM(lengths.shape, jnp.int32),
            pltpu.SMEM(spill_table.shape[::-1], jnp.int32),
            pltpu.VMEM((bs, heads, q_width), bf16),
            pltpu.VMEM(absorb_key.shape, bf16),
            pltpu.VMEM(absorb_value.shape, bf16),
            pltpu.VMEM(prefix_cache.shape[::-1], bf16),
            pltpu.VMEM((width, home), bf16),
            pltpu.VMEM((128, width), bf16),
            pltpu.VMEM((width, per_branch * block), bf16),
            pltpu.VMEM((2, bs * heads, 128), f32),
            pltpu.VMEM((latent // 128 + 1, bs * heads, 128), f32),
            pltpu.VMEM((branches, rows, width), bf16),
            pltpu.VMEM((n_ten, rows, width), bf16),
            pltpu.VMEM((branches, 16, 128), bf16),
            pltpu.VMEM((n_ten, 16, 128), bf16),
            pltpu.VMEM((n_ten * rows, 1), f32),
            pltpu.VMEM((n_ten * rows, 1), f32),
            pltpu.VMEM((n_ten * rows, latent), f32),
            pltpu.VMEM((n_ten, rows, latent), bf16),
            pltpu.VMEM((branches, rows, latent), bf16),
            pltpu.VMEM((bs * heads, v_width), f32),
            dma((8 + n_chunk,)),
            dma((n_ten,)),
            dma((n_ten,)),
            dma((n_ten,)),
            dma((n_ten,)),
            dma((n_chunk,)),
            dma((n_chunk,)),
            dma((n_chunk, n_ten)),
            dma((n_chunk, n_ten)),
            dma,
            dma,
        ]
        + [pltpu.VMEM((n_dev, wide[0], block), bf16) for wide in chunks]
        + [pltpu.VMEM((branches, wide[0], per_branch * block), bf16) for wide in chunks],
        compiler_params=pltpu.CompilerParams(
            collective_id=0, has_side_effects=True, vmem_limit_bytes=60 * 1024 * 1024
        ),
    )(
        query.reshape(bs, heads, q_width),
        absorb_key,
        absorb_value,
        prefix_cache.T,
        home_cache.swapaxes(1, 2),
        spill_pool.swapaxes(1, 2),
        new_latent,
        lengths,
        spill_table.T,
    )
    return out.reshape(branches, steps, heads, v_width)


def solution(mesh):
    in_specs = (
        P("branch", None, "tensor", None),
        P("tensor", None, None),
        P("tensor", None, None),
        P(),
        P("branch", None, None),
        P("branch", None, None),
        P("branch", None, "tensor"),
        P("branch"),
        P("branch", None),
    )
    out_specs = P("branch", None, "tensor", None)
    return jax.shard_map(
        per_device, mesh=mesh, in_specs=in_specs, out_specs=out_specs, check_vma=False
    )
```

```python
import functools
import math

import jax
import jax.numpy as jnp
from jax import lax
from jax.experimental import pallas as pl
from jax.experimental.pallas import tpu as pltpu
from jax.sharding import PartitionSpec as P

MESH = pl.DeviceIdType.MESH
FLOOR = -1e30
KEY_TILE = 512
DEPTH = 8


def nt_dot(a, b):
    return lax.dot_general(a, b, (((1,), (1,)), ((), ())), preferred_element_type=jnp.float32)


def attention_kernel(
    dims,
    query_ref,
    wk_ref,
    wv_ref,
    prefix_ref,
    home_ref,
    pool_ref,
    fresh_hbm,
    len_hbm,
    table_hbm,
    out_ref,
    fresh_ref,
    len_ref,
    table_ref,
    q_buf,
    wk_buf,
    wv_buf,
    prefix_buf,
    home_buf,
    new_buf,
    spill,
    flat_buf,
    lat_buf,
    full_send,
    full_recv,
    fresh_send,
    fresh_recv,
    peak_buf,
    mass_buf,
    acc_buf,
    lo_send,
    lo_recv,
    out_buf,
    local_sem,
    q_send_sem,
    q_recv_sem,
    f_send_sem,
    f_recv_sem,
    s_send_sem,
    s_recv_sem,
    x_send_sem,
    x_recv_sem,
    o_send_sem,
    o_recv_sem,
    *chunk_bufs,
):
    n_dev, n_ten, branches, steps, heads, nope, rope, latent, home, block, per_branch, chunks = dims
    width = latent + rope
    rows = steps * heads
    bs = branches * steps
    all_rows = n_ten * rows
    n_chunk = len(chunks)
    starts = [sum(sum(wide) for wide in chunks[:c]) * n_ten // 2 for c in range(n_chunk + 1)]
    pool_recv = chunk_bufs[:n_chunk]
    stage = chunk_bufs[n_chunk:]
    me = lax.axis_index("branch")
    mine = lax.axis_index("tensor")
    scale = (nope + rope) ** -0.5 / math.log(2.0)

    def dev(i):
        return lax.rem(me + i, n_dev)

    def ten(i):
        return lax.rem(mine + i, n_ten)

    far_first = sorted(range(1, n_ten), key=lambda i: (abs(n_ten // 2 - i), -i))

    barrier = pltpu.get_barrier_semaphore()

    def greet_dev(i, carry):
        pl.semaphore_signal(barrier, inc=1, device_id={"branch": dev(i)}, device_id_type=MESH)
        return carry

    def greet_ten(i, carry):
        pl.semaphore_signal(barrier, inc=1, device_id={"tensor": ten(i)}, device_id_type=MESH)
        return carry

    def hops(i):
        across, along = divmod(i, DEPTH)
        return min(across, n_dev // DEPTH - across) + min(along, DEPTH - along)

    for i in sorted(range(1, n_dev), key=hops, reverse=True):
        greet_dev(i, 0)
    lax.fori_loop(1, n_ten, greet_ten, 0)

    def rows_of(t, odd, c):
        first = starts[c] + odd * chunks[c][0]
        return pl.ds(pl.multiple_of(t // 2 * sum(chunks[c]) + first, 16), chunks[c][odd])

    def by_parity(body):
        for odd in range(2):
            pl.when(lax.rem(mine, 2) == odd)(functools.partial(body, odd))

    locals_ = [
        pltpu.make_async_copy(query_ref, q_buf, local_sem.at[0]),
        pltpu.make_async_copy(wk_ref, wk_buf, local_sem.at[1]),
        pltpu.make_async_copy(prefix_ref, prefix_buf, local_sem.at[2]),
        pltpu.make_async_copy(home_ref.at[mine], home_buf, local_sem.at[3]),
        pltpu.make_async_copy(wv_ref, wv_buf, local_sem.at[4]),
        pltpu.make_async_copy(fresh_hbm, fresh_ref, local_sem.at[5]),
        pltpu.make_async_copy(len_hbm, len_ref, local_sem.at[6]),
        pltpu.make_async_copy(table_hbm, table_ref, local_sem.at[7]),
    ]
    for copy in locals_:
        copy.start()

    def own_copy(odd, c):
        return pltpu.make_async_copy(
            pool_ref.at[me, rows_of(mine, odd, c)],
            pool_recv[c].at[me, pl.ds(0, chunks[c][odd])],
            local_sem.at[8 + c],
        )

    def all_blocks(odd, c, sem):
        landed = pool_recv[c].at[pl.ds(0, n_dev - 1), pl.ds(0, chunks[c][odd])]
        return pltpu.make_async_copy(landed, landed, sem.at[c])

    def block_copy(odd, c, source, target):
        return pltpu.make_async_remote_copy(
            src_ref=pool_ref.at[target, rows_of(mine, odd, c)],
            dst_ref=pool_recv[c].at[source, pl.ds(0, chunks[c][odd])],
            send_sem=s_send_sem.at[c],
            recv_sem=s_recv_sem.at[c],
            device_id={"branch": target},
            device_id_type=MESH,
        )

    locals_[0].wait()
    q_flat = q_buf[...].reshape(bs * heads, nope + rope).astype(jnp.float32)
    flat_buf[0, :, pl.ds(0, nope)] = q_flat[:, :nope]
    flat_buf[1, :, pl.ds(0, rope)] = q_flat[:, nope:]
    locals_[1].wait()
    tiles = latent // 128
    for h in range(heads):
        q_head = flat_buf[0, pl.ds(h, bs, stride=heads), :][:, :nope]
        lat_head = jnp.dot(
            q_head.astype(jnp.bfloat16), wk_buf[h], preferred_element_type=jnp.float32
        )
        for j in range(tiles):
            lat_buf[j, pl.ds(h * bs, bs), :] = lat_head[:, j * 128 : (j + 1) * 128]
        lat_buf[tiles, pl.ds(h * bs, bs), :] = flat_buf[1, pl.ds(h, bs, stride=heads), :]
    for b in range(branches):
        for s in range(steps):
            for j in range(tiles + 1):
                wide = 128 if j < tiles else rope
                full_send[b, pl.ds(s * heads, heads), pl.ds(j * 128, wide)] = lat_buf[
                    j, pl.ds(b * steps + s, heads, stride=bs), :
                ][:, :wide].astype(jnp.bfloat16)
    part = width // n_ten
    fresh_send[...] = jnp.zeros_like(fresh_send)
    locals_[5].wait()
    for b in range(branches):
        fresh_send[b, pl.ds(0, steps), pl.ds(0, part)] = fresh_ref[b]

    pl.semaphore_wait(barrier, n_dev - 1 + n_ten - 1)

    def full_copy(i, source, target):
        return pltpu.make_async_remote_copy(
            src_ref=full_send.at[target],
            dst_ref=full_recv.at[source],
            send_sem=q_send_sem.at[i],
            recv_sem=q_recv_sem.at[i],
            device_id={"tensor": target},
            device_id_type=MESH,
        )

    def fresh_copy(i, source, target):
        return pltpu.make_async_remote_copy(
            src_ref=fresh_send.at[target],
            dst_ref=fresh_recv.at[source],
            send_sem=f_send_sem.at[i],
            recv_sem=f_recv_sem.at[i],
            device_id={"tensor": target},
            device_id_type=MESH,
        )

    def send_blocks(chosen):
        @by_parity
        def _(odd):
            for c in chosen:

                def send_block(i, carry, c=c):
                    block_copy(odd, c, me, dev(i)).start()
                    return carry

                lax.fori_loop(1, n_dev, send_block, 0)
                own_copy(odd, c).start()

    send_blocks(range(1))
    for i in far_first:
        full_copy(i, mine, ten(i)).start()
        fresh_copy(i, mine, ten(i)).start()
    full_recv[mine] = full_send[mine]
    fresh_recv[mine] = fresh_send[mine]
    send_blocks(range(1, n_chunk))

    for i in range(1, n_ten):
        full_copy(i, ten(n_ten - i), mine).wait_recv()
        fresh_copy(i, ten(n_ten - i), mine).wait_recv()

    fresh_all = jnp.zeros((fresh_recv.shape[1], width + fresh_recv.shape[2]), jnp.float32)
    for t in range(n_ten):
        piece = fresh_recv[t].astype(jnp.float32)
        piece = jnp.concatenate([piece, jnp.zeros((piece.shape[0], width), jnp.float32)], 1)
        fresh_all = fresh_all + (pltpu.roll(piece, t * part, 1) if t else piece)
    new_buf[...] = jnp.zeros_like(new_buf)
    new_buf[pl.ds(0, fresh_recv.shape[1]), :] = fresh_all[:, :width].astype(jnp.bfloat16)

    queries = full_recv[...].reshape(all_rows, width)
    locals_[6].wait()
    locals_[7].wait()
    length = len_ref[mine]

    def attend(scores, combine):
        peak_old = peak_buf[...]
        peak = jnp.maximum(peak_old, jnp.max(scores, 1, keepdims=True))
        weights = jnp.exp2(scores - peak)
        factor = jnp.exp2(peak_old - peak)
        mass_buf[...] = mass_buf[...] * factor + jnp.sum(weights, 1, keepdims=True)
        peak_buf[...] = peak
        acc_buf[...] = acc_buf[...] * factor + combine(weights.astype(jnp.bfloat16))

    def attend_columns(keys, bound):
        scores = jnp.dot(queries, keys, preferred_element_type=jnp.float32) * scale
        if bound is not None:
            column = lax.broadcasted_iota(jnp.int32, scores.shape, 1)
            scores = jnp.where(column < bound, scores, FLOOR)
        attend(scores, lambda weights: nt_dot(weights, keys[:latent]))

    peak_buf[...] = jnp.full_like(peak_buf, FLOOR)
    mass_buf[...] = jnp.zeros_like(mass_buf)
    acc_buf[...] = jnp.zeros_like(acc_buf)
    locals_[2].wait()

    def prefix_tile(j, carry):
        attend_columns(prefix_buf[:, pl.ds(pl.multiple_of(j * KEY_TILE, KEY_TILE), KEY_TILE)], None)
        return carry

    lax.fori_loop(0, prefix_buf.shape[1] // KEY_TILE, prefix_tile, 0)

    def regroup_copy(i, odd, c, source, target):
        return pltpu.make_async_remote_copy(
            src_ref=stage[c].at[target, pl.ds(0, chunks[c][odd])],
            dst_ref=spill.at[rows_of(source, odd, c)],
            send_sem=x_send_sem.at[c, i],
            recv_sem=x_recv_sem.at[c, i],
            device_id={"tensor": target},
            device_id_type=MESH,
        )

    def regroup(chosen):
        @by_parity
        def _(odd):
            for c in chosen:

                all_blocks(odd, c, s_recv_sem).wait()
                own_copy(odd, c).wait()
                some = pl.ds(0, chunks[c][odd])
                for i in far_first:
                    target = ten(i)
                    for k in range(per_branch):
                        holder = table_ref[k, target] // n_dev
                        stage[c][target, some, pl.ds(k * block, block)] = pool_recv[c][holder, some, :]
                    regroup_copy(i, odd, c, mine, target).start()
                for k in range(per_branch):
                    holder = table_ref[k, mine] // n_dev
                    spill[rows_of(mine, odd, c), pl.ds(k * block, block)] = pool_recv[c][
                        holder, some, :
                    ]

    regroup(range(n_chunk - 1))

    locals_[3].wait()
    attend_columns(home_buf[...], length)
    keys = new_buf[...]
    scores = nt_dot(queries, keys) * scale
    column = lax.broadcasted_iota(jnp.int32, scores.shape, 1)
    row_step = lax.broadcasted_iota(jnp.int32, scores.shape, 0) // heads % steps
    attend(
        jnp.where(column <= row_step, scores, FLOOR),
        lambda weights: jnp.dot(weights, keys[:, :latent], preferred_element_type=jnp.float32),
    )

    regroup(range(n_chunk - 1, n_chunk))

    scores = 0.0
    for c in range(n_chunk):

        @by_parity
        def _(odd, c=c):
            for i in range(1, n_ten):
                regroup_copy(i, (odd + i) % 2, c, ten(n_ten - i), mine).wait_recv()

        span = slice(starts[c], starts[c + 1])
        scores += jnp.dot(queries[:, span], spill[span, :], preferred_element_type=jnp.float32)

    column = lax.broadcasted_iota(jnp.int32, scores.shape, 1)
    scores = jnp.where(column < length - home, scores * scale, FLOOR)
    peak_old = peak_buf[...]
    peak = jnp.maximum(peak_old, jnp.max(scores, 1, keepdims=True))
    weights = jnp.exp2(scores - peak)
    factor = jnp.exp2(peak_old - peak)
    share = 1.0 / (mass_buf[...] * factor + jnp.sum(weights, 1, keepdims=True))
    last = nt_dot(weights.astype(jnp.bfloat16), spill[pl.ds(0, latent), :])
    lo_send[...] = (
        (acc_buf[...] * (factor * share) + last * share).astype(jnp.bfloat16).reshape(lo_send.shape)
    )

    def all_back(sem):
        landed = lo_recv.at[pl.ds(0, n_ten - 1)]
        return pltpu.make_async_copy(landed, landed, sem)

    def back_copy(source, target):
        return pltpu.make_async_remote_copy(
            src_ref=lo_send.at[target],
            dst_ref=lo_recv.at[source],
            send_sem=o_send_sem,
            recv_sem=o_recv_sem,
            device_id={"tensor": target},
            device_id_type=MESH,
        )

    for i in far_first:
        back_copy(mine, ten(i)).start()
    lo_recv[mine] = lo_send[mine]
    @by_parity
    def _(odd):
        for c in range(n_chunk):

            all_blocks(odd, c, s_send_sem).wait()
            for i in range(1, n_ten):
                regroup_copy(i, odd, c, mine, ten(i)).wait_send()

    for i in range(1, n_ten):
        full_copy(i, mine, ten(i)).wait_send()
        fresh_copy(i, mine, ten(i)).wait_send()

    locals_[4].wait()
    all_back(o_recv_sem).wait()
    for j in range(tiles):
        lat_buf[j] = (
            lo_recv[:, :, pl.ds(j * 128, 128)].reshape(branches * rows, 128).astype(jnp.float32)
        )
    for h in range(heads):
        head_rows = jnp.concatenate(
            [lat_buf[j, pl.ds(h, bs, stride=heads), :] for j in range(tiles)], 1
        ).astype(jnp.bfloat16)
        out_buf[pl.ds(h, bs, stride=heads), :] = jnp.dot(
            head_rows, wv_buf[h], preferred_element_type=jnp.float32
        )
    out_ref[...] = out_buf[...].reshape(out_ref.shape).astype(jnp.bfloat16)

    all_back(o_send_sem).wait()


def per_device(
    query,
    absorb_key,
    absorb_value,
    prefix_cache,
    home_cache,
    spill_pool,
    new_latent,
    lengths,
    spill_table,
):
    branches, steps, heads, q_width = query.shape
    nope, latent = absorb_key.shape[1:]
    v_width = absorb_value.shape[2]
    rope = q_width - nope
    width = latent + rope
    home = home_cache.shape[1]
    block = spill_pool.shape[1]
    n_dev = lax.axis_size("branch")
    n_ten = lax.axis_size("tensor")
    per_branch = spill_table.shape[1]
    chunks = ((48, 48), (32, 16))
    dims = (
        n_dev, n_ten, branches, steps, heads, nope, rope, latent, home, block, per_branch, chunks
    )
    rows = steps * heads
    bs = branches * steps
    bf16, f32 = jnp.bfloat16, jnp.float32
    hbm = pl.BlockSpec(memory_space=pltpu.HBM)
    vmem = pl.BlockSpec(memory_space=pltpu.VMEM)
    dma = pltpu.SemaphoreType.DMA
    n_chunk = len(chunks)
    out = pl.pallas_call(
        functools.partial(attention_kernel, dims),
        out_shape=pltpu.VMEM((bs, heads, v_width), bf16),
        in_specs=[hbm] * 9,
        out_specs=vmem,
        scratch_shapes=[
            pltpu.VMEM(new_latent.shape, bf16),
            pltpu.SMEM(lengths.shape, jnp.int32),
            pltpu.SMEM(spill_table.shape[::-1], jnp.int32),
            pltpu.VMEM((bs, heads, q_width), bf16),
            pltpu.VMEM(absorb_key.shape, bf16),
            pltpu.VMEM(absorb_value.shape, bf16),
            pltpu.VMEM(prefix_cache.shape[::-1], bf16),
            pltpu.VMEM((width, home), bf16),
            pltpu.VMEM((128, width), bf16),
            pltpu.VMEM((width, per_branch * block), bf16),
            pltpu.VMEM((2, bs * heads, 128), f32),
            pltpu.VMEM((latent // 128 + 1, bs * heads, 128), f32),
            pltpu.VMEM((branches, rows, width), bf16),
            pltpu.VMEM((n_ten, rows, width), bf16),
            pltpu.VMEM((branches, 16, 128), bf16),
            pltpu.VMEM((n_ten, 16, 128), bf16),
            pltpu.VMEM((n_ten * rows, 1), f32),
            pltpu.VMEM((n_ten * rows, 1), f32),
            pltpu.VMEM((n_ten * rows, latent), f32),
            pltpu.VMEM((n_ten, rows, latent), bf16),
            pltpu.VMEM((branches, rows, latent), bf16),
            pltpu.VMEM((bs * heads, v_width), f32),
            dma((8 + n_chunk,)),
            dma((n_ten,)),
            dma((n_ten,)),
            dma((n_ten,)),
            dma((n_ten,)),
            dma((n_chunk,)),
            dma((n_chunk,)),
            dma((n_chunk, n_ten)),
            dma((n_chunk, n_ten)),
            dma,
            dma,
        ]
        + [pltpu.VMEM((n_dev, wide[0], block), bf16) for wide in chunks]
        + [pltpu.VMEM((branches, wide[0], per_branch * block), bf16) for wide in chunks],
        compiler_params=pltpu.CompilerParams(
            collective_id=0, has_side_effects=True, vmem_limit_bytes=60 * 1024 * 1024
        ),
    )(
        query.reshape(bs, heads, q_width),
        absorb_key,
        absorb_value,
        prefix_cache.T,
        home_cache.swapaxes(1, 2),
        spill_pool.swapaxes(1, 2),
        new_latent,
        lengths,
        spill_table.T,
    )
    return out.reshape(branches, steps, heads, v_width)


def solution(mesh):
    in_specs = (
        P("branch", None, "tensor", None),
        P("tensor", None, None),
        P("tensor", None, None),
        P(),
        P("branch", None, None),
        P("branch", None, None),
        P("branch", None, "tensor"),
        P("branch"),
        P("branch", None),
    )
    out_specs = P("branch", None, "tensor", None)
    return jax.shard_map(
        per_device, mesh=mesh, in_specs=in_specs, out_specs=out_specs, check_vma=False
    )
```

```python
import functools
import math

import jax
import jax.numpy as jnp
from jax import lax
from jax.experimental import pallas as pl
from jax.experimental.pallas import tpu as pltpu
from jax.sharding import PartitionSpec as P

MESH = pl.DeviceIdType.MESH
FLOOR = -1e30
KEY_TILE = 512
DEPTH = 8


def nt_dot(a, b):
    return lax.dot_general(a, b, (((1,), (1,)), ((), ())), preferred_element_type=jnp.float32)


def attention_kernel(
    dims,
    query_ref,
    wk_ref,
    wv_ref,
    prefix_ref,
    home_ref,
    pool_ref,
    fresh_hbm,
    len_hbm,
    table_hbm,
    out_ref,
    fresh_ref,
    len_ref,
    table_ref,
    q_buf,
    wk_buf,
    wv_buf,
    prefix_buf,
    home_buf,
    new_buf,
    spill,
    flat_buf,
    lat_buf,
    full_send,
    full_recv,
    fresh_send,
    fresh_recv,
    peak_buf,
    mass_buf,
    acc_buf,
    lo_send,
    lo_recv,
    out_buf,
    local_sem,
    q_send_sem,
    q_recv_sem,
    f_send_sem,
    f_recv_sem,
    s_send_sem,
    s_recv_sem,
    x_send_sem,
    x_recv_sem,
    o_send_sem,
    o_recv_sem,
    *chunk_bufs,
):
    n_dev, n_ten, branches, steps, heads, nope, rope, latent, home, block, per_branch, chunks = dims
    width = latent + rope
    rows = steps * heads
    bs = branches * steps
    all_rows = n_ten * rows
    n_chunk = len(chunks)
    starts = [sum(sum(wide) for wide in chunks[:c]) * n_ten // 2 for c in range(n_chunk + 1)]
    pool_recv = chunk_bufs[:n_chunk]
    stage = chunk_bufs[n_chunk:]
    me = lax.axis_index("branch")
    mine = lax.axis_index("tensor")
    scale = (nope + rope) ** -0.5 / math.log(2.0)

    def dev(i):
        return lax.rem(me + i, n_dev)

    def ten(i):
        return lax.rem(mine + i, n_ten)

    far_first = sorted(range(1, n_ten), key=lambda i: (abs(n_ten // 2 - i), -i))

    barrier = pltpu.get_barrier_semaphore()

    def greet_dev(i, carry):
        pl.semaphore_signal(barrier, inc=1, device_id={"branch": dev(i)}, device_id_type=MESH)
        return carry

    def greet_ten(i, carry):
        pl.semaphore_signal(barrier, inc=1, device_id={"tensor": ten(i)}, device_id_type=MESH)
        return carry

    def hops(i):
        across, along = divmod(i, DEPTH)
        return min(across, n_dev // DEPTH - across) + min(along, DEPTH - along)

    for i in sorted(range(1, n_dev), key=hops, reverse=True):
        greet_dev(i, 0)
    lax.fori_loop(1, n_ten, greet_ten, 0)

    def rows_of(t, odd, c):
        first = starts[c] + odd * chunks[c][0]
        return pl.ds(pl.multiple_of(t // 2 * sum(chunks[c]) + first, 16), chunks[c][odd])

    def by_parity(body):
        for odd in range(2):
            pl.when(lax.rem(mine, 2) == odd)(functools.partial(body, odd))

    locals_ = [
        pltpu.make_async_copy(query_ref, q_buf, local_sem.at[0]),
        pltpu.make_async_copy(wk_ref, wk_buf, local_sem.at[1]),
        pltpu.make_async_copy(prefix_ref, prefix_buf, local_sem.at[2]),
        pltpu.make_async_copy(home_ref.at[mine], home_buf, local_sem.at[3]),
        pltpu.make_async_copy(wv_ref, wv_buf, local_sem.at[4]),
        pltpu.make_async_copy(fresh_hbm, fresh_ref, local_sem.at[5]),
        pltpu.make_async_copy(len_hbm, len_ref, local_sem.at[6]),
        pltpu.make_async_copy(table_hbm, table_ref, local_sem.at[7]),
    ]
    for copy in locals_:
        copy.start()

    def own_copy(odd, c):
        return pltpu.make_async_copy(
            pool_ref.at[me, rows_of(mine, odd, c)],
            pool_recv[c].at[me, pl.ds(0, chunks[c][odd])],
            local_sem.at[8 + c],
        )

    def all_blocks(odd, c, sem):
        landed = pool_recv[c].at[pl.ds(0, n_dev - 1), pl.ds(0, chunks[c][odd])]
        return pltpu.make_async_copy(landed, landed, sem.at[c])

    def block_copy(odd, c, source, target):
        return pltpu.make_async_remote_copy(
            src_ref=pool_ref.at[target, rows_of(mine, odd, c)],
            dst_ref=pool_recv[c].at[source, pl.ds(0, chunks[c][odd])],
            send_sem=s_send_sem.at[c],
            recv_sem=s_recv_sem.at[c],
            device_id={"branch": target},
            device_id_type=MESH,
        )

    locals_[0].wait()
    q_flat = q_buf[...].reshape(bs * heads, nope + rope).astype(jnp.float32)
    flat_buf[0, :, pl.ds(0, nope)] = q_flat[:, :nope]
    flat_buf[1, :, pl.ds(0, rope)] = q_flat[:, nope:]
    locals_[1].wait()
    tiles = latent // 128
    for h in range(heads):
        q_head = flat_buf[0, pl.ds(h, bs, stride=heads), :][:, :nope]
        lat_head = jnp.dot(
            q_head.astype(jnp.bfloat16), wk_buf[h], preferred_element_type=jnp.float32
        )
        for j in range(tiles):
            lat_buf[j, pl.ds(h * bs, bs), :] = lat_head[:, j * 128 : (j + 1) * 128]
        lat_buf[tiles, pl.ds(h * bs, bs), :] = flat_buf[1, pl.ds(h, bs, stride=heads), :]
    for b in range(branches):
        for s in range(steps):
            for j in range(tiles + 1):
                wide = 128 if j < tiles else rope
                full_send[b, pl.ds(s * heads, heads), pl.ds(j * 128, wide)] = lat_buf[
                    j, pl.ds(b * steps + s, heads, stride=bs), :
                ][:, :wide].astype(jnp.bfloat16)
    part = width // n_ten
    fresh_send[...] = jnp.zeros_like(fresh_send)
    locals_[5].wait()
    for b in range(branches):
        fresh_send[b, pl.ds(0, steps), pl.ds(0, part)] = fresh_ref[b]

    pl.semaphore_wait(barrier, n_dev - 1 + n_ten - 1)

    def full_copy(i, source, target):
        return pltpu.make_async_remote_copy(
            src_ref=full_send.at[target],
            dst_ref=full_recv.at[source],
            send_sem=q_send_sem.at[i],
            recv_sem=q_recv_sem.at[i],
            device_id={"tensor": target},
            device_id_type=MESH,
        )

    def fresh_copy(i, source, target):
        return pltpu.make_async_remote_copy(
            src_ref=fresh_send.at[target],
            dst_ref=fresh_recv.at[source],
            send_sem=f_send_sem.at[i],
            recv_sem=f_recv_sem.at[i],
            device_id={"tensor": target},
            device_id_type=MESH,
        )

    def send_blocks(chosen):
        @by_parity
        def _(odd):
            for c in chosen:

                def send_block(i, carry, c=c):
                    block_copy(odd, c, me, dev(i)).start()
                    return carry

                lax.fori_loop(1, n_dev, send_block, 0)
                own_copy(odd, c).start()

    send_blocks(range(1))
    for i in far_first:
        full_copy(i, mine, ten(i)).start()
        fresh_copy(i, mine, ten(i)).start()
    full_recv[mine] = full_send[mine]
    fresh_recv[mine] = fresh_send[mine]
    send_blocks(range(1, n_chunk))

    for i in range(1, n_ten):
        full_copy(i, ten(n_ten - i), mine).wait_recv()
        fresh_copy(i, ten(n_ten - i), mine).wait_recv()

    fresh_all = jnp.zeros((fresh_recv.shape[1], width + fresh_recv.shape[2]), jnp.float32)
    for t in range(n_ten):
        piece = fresh_recv[t].astype(jnp.float32)
        piece = jnp.concatenate([piece, jnp.zeros((piece.shape[0], width), jnp.float32)], 1)
        fresh_all = fresh_all + (pltpu.roll(piece, t * part, 1) if t else piece)
    new_buf[...] = jnp.zeros_like(new_buf)
    new_buf[pl.ds(0, fresh_recv.shape[1]), :] = fresh_all[:, :width].astype(jnp.bfloat16)

    queries = full_recv[...].reshape(all_rows, width)
    locals_[6].wait()
    locals_[7].wait()
    length = len_ref[mine]

    def attend(scores, combine):
        peak_old = peak_buf[...]
        peak = jnp.maximum(peak_old, jnp.max(scores, 1, keepdims=True))
        weights = jnp.exp2(scores - peak)
        factor = jnp.exp2(peak_old - peak)
        mass_buf[...] = mass_buf[...] * factor + jnp.sum(weights, 1, keepdims=True)
        peak_buf[...] = peak
        acc_buf[...] = acc_buf[...] * factor + combine(weights.astype(jnp.bfloat16))

    def attend_columns(keys, bound):
        scores = jnp.dot(queries, keys, preferred_element_type=jnp.float32) * scale
        if bound is not None:
            column = lax.broadcasted_iota(jnp.int32, scores.shape, 1)
            scores = jnp.where(column < bound, scores, FLOOR)
        attend(scores, lambda weights: nt_dot(weights, keys[:latent]))

    peak_buf[...] = jnp.full_like(peak_buf, FLOOR)
    mass_buf[...] = jnp.zeros_like(mass_buf)
    acc_buf[...] = jnp.zeros_like(acc_buf)
    locals_[2].wait()

    def prefix_tile(j, carry):
        attend_columns(prefix_buf[:, pl.ds(pl.multiple_of(j * KEY_TILE, KEY_TILE), KEY_TILE)], None)
        return carry

    lax.fori_loop(0, prefix_buf.shape[1] // KEY_TILE, prefix_tile, 0)

    def regroup_copy(i, odd, c, source, target):
        return pltpu.make_async_remote_copy(
            src_ref=stage[c].at[target, pl.ds(0, chunks[c][odd])],
            dst_ref=spill.at[rows_of(source, odd, c)],
            send_sem=x_send_sem.at[c, i],
            recv_sem=x_recv_sem.at[c, i],
            device_id={"tensor": target},
            device_id_type=MESH,
        )

    holders = [[table_ref[k, ten(i)] // n_dev for k in range(per_branch)] for i in range(n_ten)]

    def regroup(chosen):
        @by_parity
        def _(odd):
            for c in chosen:

                all_blocks(odd, c, s_recv_sem).wait()
                own_copy(odd, c).wait()
                some = pl.ds(0, chunks[c][odd])
                for i in far_first:
                    target = ten(i)
                    for k, holder in enumerate(holders[i]):
                        stage[c][target, some, pl.ds(k * block, block)] = pool_recv[c][holder, some, :]
                    regroup_copy(i, odd, c, mine, target).start()
                for k, holder in enumerate(holders[0]):
                    spill[rows_of(mine, odd, c), pl.ds(k * block, block)] = pool_recv[c][
                        holder, some, :
                    ]

    regroup(range(n_chunk - 1))

    locals_[3].wait()
    attend_columns(home_buf[...], length)
    keys = new_buf[...]
    scores = nt_dot(queries, keys) * scale
    column = lax.broadcasted_iota(jnp.int32, scores.shape, 1)
    row_step = lax.broadcasted_iota(jnp.int32, scores.shape, 0) // heads % steps
    attend(
        jnp.where(column <= row_step, scores, FLOOR),
        lambda weights: jnp.dot(weights, keys[:, :latent], preferred_element_type=jnp.float32),
    )

    regroup(range(n_chunk - 1, n_chunk))

    scores = 0.0
    for c in range(n_chunk):

        @by_parity
        def _(odd, c=c):
            for i in range(1, n_ten):
                regroup_copy(i, (odd + i) % 2, c, ten(n_ten - i), mine).wait_recv()

        span = slice(starts[c], starts[c + 1])
        scores += jnp.dot(queries[:, span], spill[span, :], preferred_element_type=jnp.float32)

    column = lax.broadcasted_iota(jnp.int32, scores.shape, 1)
    scores = jnp.where(column < length - home, scores * scale, FLOOR)
    peak_old = peak_buf[...]
    peak = jnp.maximum(peak_old, jnp.max(scores, 1, keepdims=True))
    weights = jnp.exp2(scores - peak)
    factor = jnp.exp2(peak_old - peak)
    share = 1.0 / (mass_buf[...] * factor + jnp.sum(weights, 1, keepdims=True))
    last = nt_dot(weights.astype(jnp.bfloat16), spill[pl.ds(0, latent), :])
    lo_send[...] = (
        (acc_buf[...] * (factor * share) + last * share).astype(jnp.bfloat16).reshape(lo_send.shape)
    )

    def all_back(sem):
        landed = lo_recv.at[pl.ds(0, n_ten - 1)]
        return pltpu.make_async_copy(landed, landed, sem)

    def back_copy(source, target):
        return pltpu.make_async_remote_copy(
            src_ref=lo_send.at[target],
            dst_ref=lo_recv.at[source],
            send_sem=o_send_sem,
            recv_sem=o_recv_sem,
            device_id={"tensor": target},
            device_id_type=MESH,
        )

    for i in far_first:
        back_copy(mine, ten(i)).start()
    lo_recv[mine] = lo_send[mine]
    @by_parity
    def _(odd):
        for c in range(n_chunk):

            all_blocks(odd, c, s_send_sem).wait()
            for i in range(1, n_ten):
                regroup_copy(i, odd, c, mine, ten(i)).wait_send()

    for i in range(1, n_ten):
        full_copy(i, mine, ten(i)).wait_send()
        fresh_copy(i, mine, ten(i)).wait_send()

    locals_[4].wait()
    all_back(o_recv_sem).wait()
    for j in range(tiles):
        lat_buf[j] = (
            lo_recv[:, :, pl.ds(j * 128, 128)].reshape(branches * rows, 128).astype(jnp.float32)
        )
    for h in range(heads):
        head_rows = jnp.concatenate(
            [lat_buf[j, pl.ds(h, bs, stride=heads), :] for j in range(tiles)], 1
        ).astype(jnp.bfloat16)
        out_buf[pl.ds(h, bs, stride=heads), :] = jnp.dot(
            head_rows, wv_buf[h], preferred_element_type=jnp.float32
        )
    out_ref[...] = out_buf[...].reshape(out_ref.shape).astype(jnp.bfloat16)

    all_back(o_send_sem).wait()


def per_device(
    query,
    absorb_key,
    absorb_value,
    prefix_cache,
    home_cache,
    spill_pool,
    new_latent,
    lengths,
    spill_table,
):
    branches, steps, heads, q_width = query.shape
    nope, latent = absorb_key.shape[1:]
    v_width = absorb_value.shape[2]
    rope = q_width - nope
    width = latent + rope
    home = home_cache.shape[1]
    block = spill_pool.shape[1]
    n_dev = lax.axis_size("branch")
    n_ten = lax.axis_size("tensor")
    per_branch = spill_table.shape[1]
    chunks = ((48, 48), (32, 16))
    dims = (
        n_dev, n_ten, branches, steps, heads, nope, rope, latent, home, block, per_branch, chunks
    )
    rows = steps * heads
    bs = branches * steps
    bf16, f32 = jnp.bfloat16, jnp.float32
    hbm = pl.BlockSpec(memory_space=pltpu.HBM)
    vmem = pl.BlockSpec(memory_space=pltpu.VMEM)
    dma = pltpu.SemaphoreType.DMA
    n_chunk = len(chunks)
    out = pl.pallas_call(
        functools.partial(attention_kernel, dims),
        out_shape=pltpu.VMEM((bs, heads, v_width), bf16),
        in_specs=[hbm] * 9,
        out_specs=vmem,
        scratch_shapes=[
            pltpu.VMEM(new_latent.shape, bf16),
            pltpu.SMEM(lengths.shape, jnp.int32),
            pltpu.SMEM(spill_table.shape[::-1], jnp.int32),
            pltpu.VMEM((bs, heads, q_width), bf16),
            pltpu.VMEM(absorb_key.shape, bf16),
            pltpu.VMEM(absorb_value.shape, bf16),
            pltpu.VMEM(prefix_cache.shape[::-1], bf16),
            pltpu.VMEM((width, home), bf16),
            pltpu.VMEM((128, width), bf16),
            pltpu.VMEM((width, per_branch * block), bf16),
            pltpu.VMEM((2, bs * heads, 128), f32),
            pltpu.VMEM((latent // 128 + 1, bs * heads, 128), f32),
            pltpu.VMEM((branches, rows, width), bf16),
            pltpu.VMEM((n_ten, rows, width), bf16),
            pltpu.VMEM((branches, 16, 128), bf16),
            pltpu.VMEM((n_ten, 16, 128), bf16),
            pltpu.VMEM((n_ten * rows, 1), f32),
            pltpu.VMEM((n_ten * rows, 1), f32),
            pltpu.VMEM((n_ten * rows, latent), f32),
            pltpu.VMEM((n_ten, rows, latent), bf16),
            pltpu.VMEM((branches, rows, latent), bf16),
            pltpu.VMEM((bs * heads, v_width), f32),
            dma((8 + n_chunk,)),
            dma((n_ten,)),
            dma((n_ten,)),
            dma((n_ten,)),
            dma((n_ten,)),
            dma((n_chunk,)),
            dma((n_chunk,)),
            dma((n_chunk, n_ten)),
            dma((n_chunk, n_ten)),
            dma,
            dma,
        ]
        + [pltpu.VMEM((n_dev, wide[0], block), bf16) for wide in chunks]
        + [pltpu.VMEM((branches, wide[0], per_branch * block), bf16) for wide in chunks],
        compiler_params=pltpu.CompilerParams(
            collective_id=0, has_side_effects=True, vmem_limit_bytes=60 * 1024 * 1024
        ),
    )(
        query.reshape(bs, heads, q_width),
        absorb_key,
        absorb_value,
        prefix_cache.T,
        home_cache.swapaxes(1, 2),
        spill_pool.swapaxes(1, 2),
        new_latent,
        lengths,
        spill_table.T,
    )
    return out.reshape(branches, steps, heads, v_width)


def solution(mesh):
    in_specs = (
        P("branch", None, "tensor", None),
        P("tensor", None, None),
        P("tensor", None, None),
        P(),
        P("branch", None, None),
        P("branch", None, None),
        P("branch", None, "tensor"),
        P("branch"),
        P("branch", None),
    )
    out_specs = P("branch", None, "tensor", None)
    return jax.shard_map(
        per_device, mesh=mesh, in_specs=in_specs, out_specs=out_specs, check_vma=False
    )
```
